512 devices in a mesh: dp: 128 (over x, z_lo, y, core), mp: 4 (over z_hi).
Axes of the slice: x: 4, y: 4, z: 16 (z_hi: 4, z_lo: 4; z = z_hi * 4 + z_lo), core: 2. Of those that a mesh axis runs over, the one named last changes fastest.
Arguments:
- query_embedding_cache: bfloat16 [128, 4096], P('dp'), may hold values from -0.1 to 0.1
- passage_embedding_cache: bfloat16 [128, 4096], P('dp'), may hold values from -0.099609375 to 0.099609375
- positive: int32 [128], P('dp'), may hold values from 0 to 127, as said below
- attention_head_outputs: bfloat16 [65536, 4096], P('dp', 'mp'), may hold values from -6 to 6
- residual: bfloat16 [65536, 4096], P('dp', 'mp'), may hold values from -16 to 16
- output_projection_weight: bfloat16 [4096, 4096], P('dp', 'mp'), may hold values from -0.375 to 0.375
- final_norm_gain: float32 [4096], P('mp'), may hold values from 0.1 to 1.9
- adapter_down_weight: bfloat16 [16, 4096], replicated, may hold values from -0.09375 to 0.09375
- adapter_up_weight: bfloat16 [16, 4096], P(None, 'mp'), may hold values from -1.5 to 1.5
- sequence_length: int32 [128], P('dp'), may hold values from 64 to 512
Outputs:
- query_grad: float32 [128, 4096], P('dp')
- passage_grad: float32 [128, 4096], P('dp')
- down_grad: float32 [16, 4096], P(None, ('mp', 'dp'))
- up_grad: float32 [16, 4096], P(None, ('mp', 'dp'))
The draws below stay inside these ranges and needn't reach their ends.
Inputs may be any that keep to these rules, and one draw needn't show every extreme that they name: Each passage is the positive of exactly one query.
All inputs are finite; a program needn't handle non-finite values.
Results may differ from the reference program's by a relative error of at most 0.0009.
The reference program's roundings to bfloat16 on the way count: a program that leaves them out, or rounds other values in their place, can miss the bound.
Values may be sent and summed in bfloat16 or wider, within the bound.
No kernel may reach another device: no remote copies, remote signals or barrier semaphores. Data moves between devices by JAX's collectives and lax.ppermute only.
A program may use at most 64 MiB of HBM per device.

```python
import jax
import jax.numpy as jnp
from jax import lax

MODEL_WIDTH = 4096
L = 512
ADAPTER_RANK = 16
PAIRS_DEV = 1
PAIRS = 128
TOKENS = 65536
N_DP = 128


def shared_pairs(key):
    normal_draws = jax.random.normal(jax.random.fold_in(key, 101), (PAIRS, MODEL_WIDTH), jnp.float32)
    queries = 0.015625 * jnp.clip(normal_draws, -6.4, 6.4)
    pairing = jax.random.permutation(jax.random.fold_in(key, 102), PAIRS).astype(jnp.int32)
    return (queries, pairing)


def draw_query_embedding_cache(key, part):
    queries, pairing = shared_pairs(key)
    return queries.astype(jnp.bfloat16)


def draw_positive(key, part):
    queries, pairing = shared_pairs(key)
    return pairing


def draw_residual(key, part):
    queries, pairing = shared_pairs(key)
    key = jax.random.fold_in(key, 5)
    owners = jnp.argsort(pairing).astype(jnp.int32)
    chosen = jnp.take(queries, owners[::PAIRS_DEV], axis=0) * 128.0
    noise_part = 0.5 * jnp.clip(jax.random.normal(key, (N_DP, L, MODEL_WIDTH), jnp.float32), -6.0, 6.0)
    combined = noise_part + chosen[:, None, :]
    return combined.reshape(N_DP * L, MODEL_WIDTH).astype(jnp.bfloat16)


def place_ends(drawn, rng, smallest, high):
    shape = drawn.shape
    spot = [jax.random.randint(jax.random.fold_in(rng, axis), (), 0, shape[axis]) for axis in range(len(shape))]
    drawn = drawn.at[tuple(spot)].set(smallest)
    longest = shape.index(max(shape))
    spot[longest] = (spot[longest] + 1) % shape[longest]
    return drawn.at[tuple(spot)].set(high)


def raised(drawn, stream_key, source, target, parts, factor):
    def block_of(axis_at):
        return (jnp.arange(drawn.shape[axis_at]) // (drawn.shape[axis_at] // parts)).reshape((-1,) + (1,) * (drawn.ndim - 1 - axis_at))

    one_side = jax.random.permutation(stream_key, parts)[block_of(target)]
    second = (block_of(target) + parts // 2) % parts
    return jnp.where((block_of(source) == one_side) | (block_of(source) == second), factor * drawn, drawn)


def steps_of(rng, dims, pieces, smallest, largest):
    level = 1.0
    for dim, parts in pieces:
        draws = jax.random.uniform(jax.random.fold_in(jax.random.fold_in(rng, 6), dim), (parts,), jnp.float32, smallest / len(pieces), largest / len(pieces))
        level = level * jnp.repeat(jnp.exp(draws), dims[dim] // parts).reshape((-1,) + (1,) * (len(dims) - 1 - dim))
    return level


def noise(own_key, shape, spread, limit, split=(), kind=jnp.bfloat16):
    drawn = jax.random.normal(own_key, shape, jnp.float32) * spread
    if len(split) > 0:
        drawn = steps_of(own_key, shape, split, -0.22, 0.18) * drawn
    return jnp.clip(drawn, min=-limit, max=limit).astype(kind)


def bell_draw_with(rng, shape, scale, bound, cuts, heavy, kind=jnp.bfloat16):
    entries = scale * jax.random.normal(rng, shape, jnp.float32)
    if cuts:
        entries = entries * steps_of(rng, shape, cuts, -0.22, 0.18)
    return jnp.clip(raised(entries, jax.random.fold_in(rng, 3), *heavy), -bound, bound).astype(kind)


def setup_inputs(seed: int = 0) -> dict:
    streams_of = jax.random.split(jax.random.key(seed), 11)
    query_embedding_cache = draw_query_embedding_cache(jax.random.fold_in(streams_of[10], 71), 0)
    passage_embedding_cache = noise(streams_of[1], (PAIRS, MODEL_WIDTH), 0.015625, 0.099609375, ((0, 128),))
    positive = draw_positive(jax.random.fold_in(streams_of[10], 71), 0)
    attention_head_outputs = noise(streams_of[3], (TOKENS, MODEL_WIDTH), 1.0, 6.0, ((0, 128), (1, 4)))
    residual = draw_residual(jax.random.fold_in(streams_of[10], 71), 0)
    output_projection_weight = bell_draw_with(streams_of[5], (MODEL_WIDTH, MODEL_WIDTH), MODEL_WIDTH ** -0.5, 0.375, ((0, 128), (1, 4)), (0, 1, 128, 5.5))
    final_norm_gain = jnp.clip(1.0 + 0.18 * jax.random.normal(streams_of[6], (MODEL_WIDTH,), jnp.float32), 0.1, 1.9)
    adapter_down_weight = noise(streams_of[7], (ADAPTER_RANK, MODEL_WIDTH), MODEL_WIDTH ** -0.5, 0.09375)
    adapter_up_weight = noise(streams_of[8], (ADAPTER_RANK, MODEL_WIDTH), ADAPTER_RANK ** -0.5, 1.5, ((1, 4),))
    sequence_length = place_ends(jax.random.randint(streams_of[9], (N_DP,), L // 8, L + 1), jax.random.fold_in(streams_of[9], 1), L // 8, L).astype(jnp.int32)
    return dict(query_embedding_cache=query_embedding_cache, passage_embedding_cache=passage_embedding_cache, positive=positive, attention_head_outputs=attention_head_outputs, residual=residual, output_projection_weight=output_projection_weight, final_norm_gain=final_norm_gain, adapter_down_weight=adapter_down_weight, adapter_up_weight=adapter_up_weight, sequence_length=sequence_length)


logit_divisor = 0.02
unit_floor = 1e-06
norm_floor = 1e-05

def unit_rows(rows):
    wide = rows.astype(jnp.float32)
    scale = 1.0 / jnp.sqrt(lax.optimization_barrier(jnp.sum(wide * wide, axis=1, keepdims=True)) + unit_floor)
    return (wide * scale, scale)

def reference(query_embedding_cache, passage_embedding_cache, positive, attention_head_outputs, residual, output_projection_weight, final_norm_gain, adapter_down_weight, adapter_up_weight, sequence_length):
    query_unit, query_scale = unit_rows(query_embedding_cache)
    passage_unit, passage_scale = unit_rows(passage_embedding_cache)
    question_portion = query_unit.astype(jnp.bfloat16)
    document_portion = passage_unit.astype(jnp.bfloat16)
    similarity_table = jnp.dot(question_portion, document_portion.T, preferred_element_type=jnp.float32) / logit_divisor
    partition_function = jnp.log(lax.optimization_barrier(jnp.sum(jnp.exp(similarity_table), axis=1)))
    columns = jnp.arange(PAIRS, dtype=jnp.int32)
    positive_label = (columns[None, :] == positive[:, None]).astype(jnp.float32)
    normalized_probability = ((jnp.exp(similarity_table - partition_function[:, None]) - positive_label) / logit_divisor).astype(jnp.bfloat16)
    query_dir = jnp.dot(normalized_probability, document_portion, preferred_element_type=jnp.float32)
    passage_dir = jnp.dot(normalized_probability.T, question_portion, preferred_element_type=jnp.float32)
    query_grad = (query_dir - query_unit * lax.optimization_barrier(jnp.sum(query_unit * query_dir, axis=1, keepdims=True))) * query_scale
    passage_grad = (passage_dir - passage_unit * lax.optimization_barrier(jnp.sum(passage_unit * passage_dir, axis=1, keepdims=True))) * passage_scale
    upstream = passage_grad[::PAIRS_DEV]
    heads_all = attention_head_outputs.reshape(N_DP, L, MODEL_WIDTH)
    resid_all = residual.reshape(N_DP, L, MODEL_WIDTH)
    gain = final_norm_gain.astype(jnp.float32)
    up_weight_wide = adapter_up_weight.astype(jnp.float32)
    positions = jnp.arange(L, dtype=jnp.int32)

    def encode_sequence(packed):
        head_outputs, residual_state, upper, length = packed
        projected_output = jnp.dot(head_outputs, output_projection_weight, preferred_element_type=jnp.float32)
        lowrank_input = jnp.dot(head_outputs, adapter_down_weight.T, preferred_element_type=jnp.float32)
        lowrank_input_half = lowrank_input.astype(jnp.bfloat16)
        hidden_state = residual_state.astype(jnp.float32) + projected_output + 2.0 * jnp.dot(lowrank_input_half, adapter_up_weight, preferred_element_type=jnp.float32)
        inverse = 1.0 / jnp.sqrt(lax.optimization_barrier(jnp.mean(hidden_state * hidden_state, axis=1)) + norm_floor)
        scaled = gain * upper
        dot_row = jnp.dot(hidden_state, scaled, precision=lax.Precision.HIGHEST)
        mask = (positions < length).astype(jnp.float32) / length.astype(jnp.float32)
        hidden_grad = mask[:, None] * (scaled[None, :] * inverse[:, None] - hidden_state * (inverse ** 3 * dot_row / MODEL_WIDTH)[:, None])
        low_grad = 2.0 * jnp.dot(hidden_grad, up_weight_wide.T, precision=lax.Precision.HIGHEST)
        low_grad_bf = low_grad.astype(jnp.bfloat16)
        down_term = jnp.dot(low_grad_bf.T, head_outputs, preferred_element_type=jnp.float32)
        up_term = 2.0 * jnp.dot(lowrank_input_half.astype(jnp.float32).T, hidden_grad, precision=lax.Precision.HIGHEST)
        return (down_term, up_term)
    down_terms, up_terms = lax.map(encode_sequence, (heads_all, resid_all, upstream, sequence_length))
    down_grad = lax.optimization_barrier(jnp.sum(down_terms, axis=0))
    up_grad = lax.optimization_barrier(jnp.sum(up_terms, axis=0))
    return (query_grad, passage_grad, down_grad, up_grad)
```

```python
import jax
import jax.numpy as jnp
from jax import lax
from jax.experimental import pallas as pl
from jax.experimental.pallas import tpu as pltpu
from jax.sharding import Mesh, PartitionSpec as P

logit_divisor = 0.02
unit_floor = 1e-06
norm_floor = 1e-05
AXES = ("x", "zl", "y", "core", "mp")
SIZES = (4, 4, 4, 2, 4)
DP = AXES[:4]
f32 = jnp.float32
bf16 = jnp.bfloat16


def ring(step):
    return [(i, (i + step) % 4) for i in range(4)]


def dot(left, right, dims, precision=None):
    return lax.dot_general(
        left, right, (dims, ((), ())), precision=precision, preferred_element_type=f32
    )


def gather(rows, axes):
    return lax.all_gather(rows, axes, axis=0, tiled=True)


def spread(rows, axis, size):
    copies = jnp.broadcast_to(rows[None], (size,) + rows.shape)
    return lax.all_to_all(copies, axis, 0, 0, tiled=True).reshape(-1, rows.shape[1])


def unit_rows(rows):
    wide = rows.astype(f32)
    scale = lax.rsqrt(jnp.sum(wide * wide, axis=1, keepdims=True) + unit_floor)
    return (wide * scale, scale)


def gather_line(weight, query, passage, positive):
    tail = jnp.concatenate(
        [
            query.reshape(8, 512),
            passage.reshape(8, 512),
            jnp.broadcast_to(positive.astype(bf16)[:, None], (2, 512)),
        ]
    )
    parts = [jnp.concatenate([weight[:, :512], tail]), jnp.concatenate([weight[:, 512:], tail])]
    sent = jnp.stack(parts * 4)
    line = lax.all_to_all(sent, ("zl", "core"), 0, 0, tiled=True)
    pairs = jnp.concatenate([line[:, 32:48].reshape(8, 8192), line[:, 48, :128]], axis=1)
    return line[:, :32].reshape(4, 64, 512), pairs


def pair_grads(query, passage, packed):
    queries, passages = packed[:, :4096], packed[:, 4096:8192]
    targets = packed[:, 8192:8193].astype(f32)
    place = lax.broadcasted_iota(jnp.int32, (1, 128), 1)
    x, y, zl, core = place // 32, (place // 8) % 4, (place // 2) % 4, place % 2
    ids = (((x * 4 + zl) * 4 + y) * 2 + core).astype(f32)
    query_unit, _ = unit_rows(queries)
    passage_unit, _ = unit_rows(passages)
    query_bf, passage_bf = query_unit.astype(bf16), passage_unit.astype(bf16)
    scores = dot(query_bf, passage_bf, ((1,), (1,))) / logit_divisor
    row_total = jnp.log(jnp.sum(jnp.exp(scores), axis=1, keepdims=True))
    label = (targets == ids).astype(f32)
    weights = ((jnp.exp(scores - row_total) - label) / logit_divisor).astype(bf16)
    me = lax.axis_index(("x", "y", "zl", "core"))
    own_row = lax.dynamic_slice_in_dim(weights, me, 1, 0)
    own_col = jnp.sum(
        jnp.where(place == me, weights.astype(f32), 0.0), axis=1, keepdims=True
    ).astype(bf16)
    query_dir = dot(own_row, passage_bf, ((1,), (0,)))
    passage_dir = dot(own_col, query_bf, ((0,), (0,)))

    def project(rows, direction):
        unit, scale = unit_rows(rows)
        return (direction - unit * jnp.sum(unit * direction, axis=1, keepdims=True)) * scale

    return project(query, query_dir), project(passage, passage_dir)


def gather_near(part):
    return lax.ppermute(part, "mp", ring(1)), lax.ppermute(part, "mp", ring(3))


def gather_far(before, after):
    cut = before.shape[0] // 2
    left = lax.ppermute(before[:cut], "mp", ring(1))
    right = lax.ppermute(after[cut:], "mp", ring(3))
    return jnp.stack([before, after, jnp.concatenate([left, right])])


def gather_valid(part, count):
    tokens, cols = part.shape

    def prefix(size):
        def branch(rows):
            if size == 0:
                return jnp.zeros((3, tokens, cols), rows.dtype)
            blocks = gather_far(*gather_near(rows[:size]))
            return jnp.pad(blocks, ((0, 0), (0, tokens - size), (0, 0)))

        return branch

    return lax.switch(count, [prefix(size) for size in range(0, tokens + 1, 64)], part)


def split(values):
    high = values.astype(bf16)
    return high, (values - high.astype(f32)).astype(bf16)


def hidden_kernel(
    place_ref, heads_ref, first_ref, second_ref, own_ref, other_ref, resid_ref, down_ref, up_ref,
    rows_ref, hidden_ref, low_ref, stats_ref, heads, weights, stats, sems
):
    mp, core = place_ref[0], place_ref[1]
    tokens, cols = heads_ref.shape
    cut = first_ref.shape[1]
    copies = []
    for i in range(4):
        at = pl.ds(pl.multiple_of(lax.rem(mp + (0, 3, 1, 2)[i], 4) * cols, cols), cols)
        if i == 0:
            copies.append(pltpu.make_async_copy(heads_ref, heads.at[:, at], sems.at[4]))
            continue
        for k, ref in enumerate((first_ref, second_ref)):
            part = heads.at[pl.ds(k * cut, cut), at]
            copies.append(pltpu.make_async_copy(ref.at[i - 1], part, sems.at[3 + 2 * i + k]))
    early = len(copies)
    for i in range(4):
        ref = own_ref if i < 2 else other_ref
        part = ref.at[:, :, :, pl.ds((i % 2) * 256, 256)]
        copies.append(pltpu.make_async_copy(part, weights.at[i], sems.at[i]))
    for copy in copies:
        copy.start()
    for copy in copies[:early]:
        copy.wait()

    low = dot(down_ref[...], heads[...], ((1,), (1,)))
    low_bf = low.astype(bf16)
    low_ref[...] = low_bf
    stats[...] = jnp.zeros_like(stats)

    @pl.loop(0, 4)
    def _(step):
        pltpu.make_async_copy(weights.at[step], weights.at[step], sems.at[step]).wait()
        half = jnp.where(step < 2, core, 1 - core)
        at = pl.multiple_of(half * 512 + lax.rem(step, 2) * 256, 256)
        columns = pl.ds(at, 256)
        total = resid_ref[:, columns].astype(f32) + 2.0 * dot(
            low_bf, up_ref[:, columns], ((0,), (0,))
        )
        rows = jnp.concatenate(
            [
                weights[step, x * 4 + y, zl]
                for x in range(4)
                for zl in range(4)
                for y in range(4)
            ]
        )
        proj = dot(heads[...], rows, ((1,), (0,)))
        total += proj
        hidden_ref[:, columns] = total
        high, rest = split(total)
        row_high, row_rest = split(rows_ref[columns, :])
        inner = ((1,), (0,))
        products = dot(high, row_high, inner) + (
            dot(high, row_rest, inner) + dot(rest, row_high, inner)
        )
        square = total * total
        lane = lax.broadcasted_iota(jnp.int32, (tokens, 128), 1)
        sums = square[:, :128] + square[:, 128:]
        stats[...] += products + jnp.where(
            lane == 0, jnp.sum(sums, axis=1, keepdims=True), 0.0
        )

    stats_ref[...] = stats[...].T[:24]


def hidden_and_stats(place, heads, first, second, own, other, resid, down, up, rows):
    tokens, cols = heads.shape
    vmem = pl.BlockSpec(memory_space=pltpu.VMEM)
    hbm = pl.BlockSpec(memory_space=pl.ANY)
    smem = pl.BlockSpec(memory_space=pltpu.SMEM)
    return pl.pallas_call(
        hidden_kernel,
        out_shape=(
            jax.ShapeDtypeStruct((tokens, cols), f32),
            jax.ShapeDtypeStruct((16, tokens), bf16),
            jax.ShapeDtypeStruct((24, tokens), f32),
        ),
        in_specs=[smem] + [hbm] * 5 + [vmem] * 4,
        out_specs=(vmem, vmem, vmem),
        scratch_shapes=[
            pltpu.VMEM((tokens, 4 * cols), bf16),
            pltpu.VMEM((4, 16, 4, 64, 256), bf16),
            pltpu.VMEM((tokens, 128), f32),
            pltpu.SemaphoreType.DMA((11,)),
        ],
        compiler_params=pltpu.CompilerParams(vmem_limit_bytes=48 * 1024 * 1024),
        cost_estimate=pl.CostEstimate(
            flops=2 * tokens * 4096 * cols, bytes_accessed=16 * 2**20, transcendentals=0
        ),
    )(place, heads, first, second, own, other, resid, down, up, rows)


def shards(
    query_embedding_cache,
    passage_embedding_cache,
    positive,
    heads,
    residual,
    output_projection_weight,
    final_norm_gain,
    adapter_down_weight,
    adapter_up_weight,
    sequence_length,
):
    tokens, cols = heads.shape
    width = adapter_down_weight.shape[1]
    mp = lax.axis_index("mp")
    core = lax.axis_index("core")
    length = sequence_length[0]
    cut = tokens // 2
    near = gather_near(heads[:cut])
    line, pairs = gather_line(
        output_projection_weight, query_embedding_cache, passage_embedding_cache, positive
    )
    own = gather(line, ("x", "y")).reshape(16, 4, 64, 512)
    packed = spread(pairs, ("x", "y"), 16)
    near, packed = lax.optimization_barrier((near, packed))
    query_grad, passage_grad = pair_grads(
        query_embedding_cache, passage_embedding_cache, packed
    )
    first = gather_far(*near)
    own, first, passage_grad = lax.optimization_barrier((own, first, passage_grad))
    count = jnp.clip((length - cut + 63) // 64, 0, cut // 64)
    rest = lax.optimization_barrier((heads[cut:], first))[0]
    second = gather_valid(rest, count)
    other = lax.ppermute(own, "core", [(0, 1), (1, 0)])
    upper = lax.dynamic_slice_in_dim(passage_grad, mp * cols, cols, 1)
    scaled = final_norm_gain[None, :] * upper

    up_wide = adapter_up_weight.astype(f32)
    scaled_up = jnp.sum(up_wide * scaled, axis=1)[None, :]
    hidden, low_bf, stats = hidden_and_stats(
        jnp.stack([mp, core]).astype(jnp.int32),
        heads,
        first,
        second,
        own,
        other,
        residual,
        adapter_down_weight,
        adapter_up_weight,
        jnp.pad(jnp.concatenate([scaled, up_wide]), ((1, 110), (0, 0))).T,
    )
    stats = jnp.concatenate(
        [
            stats[0:18],
            jnp.pad(scaled_up, ((0, 0), (0, tokens - 16))),
            jnp.zeros((5, tokens), f32),
        ]
    )
    stats = jnp.sum(spread(stats, "mp", 4).reshape(4, 24, tokens), axis=0)
    sumsq, dot_row, hidden_up = stats[0:1], stats[1:2], stats[2:18]
    scaled_up = stats[18, :16][:, None]
    inverse = lax.rsqrt(sumsq / width + norm_floor)
    factor = inverse**3 * dot_row / width
    positions = lax.broadcasted_iota(jnp.int32, (1, tokens), 1)
    mask = (positions < length).astype(f32) / length.astype(f32)
    low_grad = 2.0 * mask * (scaled_up * inverse - hidden_up * factor)
    down_term = dot(heads, low_grad.astype(bf16), ((0,), (1,)))
    low_wide = low_bf.astype(f32)
    hidden_grad = mask.reshape(tokens, 1) * (
        scaled * inverse.reshape(tokens, 1) - hidden * factor.reshape(tokens, 1)
    )
    up_term = 2.0 * dot(hidden_grad, low_wide, ((0,), (1,)), lax.Precision.HIGHEST)
    terms = jnp.concatenate([down_term, up_term], axis=1).reshape(128, 8, 32)
    terms = lax.all_to_all(terms, ("x", "zl"), 0, 0, tiled=True)
    terms = jnp.sum(terms.reshape(16, 8, 8, 32), axis=0)
    terms = jnp.sum(lax.all_to_all(terms, ("y", "core"), 0, 0, tiled=True), axis=0)
    return query_grad, passage_grad, terms[:, :16].T, terms[:, 16:].T


def solution(mesh):
    fine = Mesh(mesh.devices.reshape(SIZES), AXES)
    both = P(DP, "mp")
    placed = (
        P(DP, None),
        P(DP, None),
        P(DP),
        both,
        both,
        both,
        P("mp"),
        P(),
        P(None, "mp"),
        P(DP),
    )
    last = P(None, ("mp",) + DP)
    return jax.shard_map(
        shards,
        mesh=fine,
        in_specs=placed,
        out_specs=(P(DP, None), P(DP, None), last, last),
        check_vma=False,
    )
```

```python
import jax
import jax.numpy as jnp
from jax import lax
from jax.experimental import pallas as pl
from jax.experimental.pallas import tpu as pltpu
from jax.sharding import Mesh, PartitionSpec as P

logit_divisor = 0.02
unit_floor = 1e-06
norm_floor = 1e-05
AXES = ("x", "zl", "y", "core", "mp")
SIZES = (4, 4, 4, 2, 4)
DP = AXES[:4]
f32 = jnp.float32
bf16 = jnp.bfloat16


def ring(step):
    return [(i, (i + step) % 4) for i in range(4)]


def dot(left, right, dims, precision=None):
    return lax.dot_general(
        left, right, (dims, ((), ())), precision=precision, preferred_element_type=f32
    )


def gather(rows, axes):
    return lax.all_gather(rows, axes, axis=0, tiled=True)


def spread(rows, axis, size):
    copies = jnp.broadcast_to(rows[None], (size,) + rows.shape)
    return lax.all_to_all(copies, axis, 0, 0, tiled=True).reshape(-1, rows.shape[1])


def unit_rows(rows):
    wide = rows.astype(f32)
    scale = lax.rsqrt(jnp.sum(wide * wide, axis=1, keepdims=True) + unit_floor)
    return (wide * scale, scale)


def gather_line(weight, query, passage, positive):
    tail = jnp.concatenate(
        [
            query.reshape(8, 512),
            passage.reshape(8, 512),
            jnp.broadcast_to(positive.astype(bf16)[:, None], (2, 512)),
        ]
    )
    parts = [jnp.concatenate([weight[:, :512], tail]), jnp.concatenate([weight[:, 512:], tail])]
    sent = jnp.stack(parts * 4)
    line = lax.all_to_all(sent, ("zl", "core"), 0, 0, tiled=True)
    pairs = jnp.concatenate([line[:, 32:48].reshape(8, 8192), line[:, 48, :128]], axis=1)
    return line[:, :32].reshape(4, 64, 512), pairs


def pair_grads(query, passage, packed):
    queries, passages = packed[:, :4096], packed[:, 4096:8192]
    targets = packed[:, 8192:8193].astype(f32)
    place = lax.broadcasted_iota(jnp.int32, (1, 128), 1)
    x, y, zl, core = place // 32, (place // 8) % 4, (place // 2) % 4, place % 2
    ids = (((x * 4 + zl) * 4 + y) * 2 + core).astype(f32)
    query_unit, _ = unit_rows(queries)
    passage_unit, _ = unit_rows(passages)
    query_bf, passage_bf = query_unit.astype(bf16), passage_unit.astype(bf16)
    scores = dot(query_bf, passage_bf, ((1,), (1,))) / logit_divisor
    row_total = jnp.log(jnp.sum(jnp.exp(scores), axis=1, keepdims=True))
    label = (targets == ids).astype(f32)
    weights = ((jnp.exp(scores - row_total) - label) / logit_divisor).astype(bf16)
    me = lax.axis_index(("x", "y", "zl", "core"))
    own_row = lax.dynamic_slice_in_dim(weights, me, 1, 0)
    own_col = jnp.sum(
        jnp.where(place == me, weights.astype(f32), 0.0), axis=1, keepdims=True
    ).astype(bf16)
    query_dir = dot(own_row, passage_bf, ((1,), (0,)))
    passage_dir = dot(own_col, query_bf, ((0,), (0,)))

    def project(rows, direction):
        unit, scale = unit_rows(rows)
        return (direction - unit * jnp.sum(unit * direction, axis=1, keepdims=True)) * scale

    return project(query, query_dir), project(passage, passage_dir)


def gather_near(part):
    return lax.ppermute(part, "mp", ring(1)), lax.ppermute(part, "mp", ring(3))


def gather_far(before, after):
    cut = before.shape[0] // 2
    left = lax.ppermute(before[:cut], "mp", ring(1))
    right = lax.ppermute(after[cut:], "mp", ring(3))
    return jnp.stack([before, after, jnp.concatenate([left, right])])


def gather_valid(part, count, step):
    tokens, cols = part.shape

    def prefix(size):
        def branch(rows):
            blocks = gather_far(*gather_near(rows[:size]))
            return jnp.pad(blocks, ((0, 0), (0, tokens - size), (0, 0)))

        return branch

    sizes = range(step, tokens + 1, step)
    return lax.switch(count - 1, [prefix(size) for size in sizes], part)


def split(values):
    high = values.astype(bf16)
    return high, (values - high.astype(f32)).astype(bf16)


def hidden_kernel(
    place_ref, heads_ref, blocks_ref, own_ref, other_ref, resid_ref, down_ref, up_ref,
    rows_ref, hidden_ref, low_ref, stats_ref, heads, weights, stats, sems
):
    mp, core = place_ref[0], place_ref[1]
    tokens, cols = heads_ref.shape
    copies = []
    for i in range(4):
        at = pl.ds(pl.multiple_of(lax.rem(mp + (0, 3, 1, 2)[i], 4) * cols, cols), cols)
        source = blocks_ref.at[i - 1] if i else heads_ref
        copies.append(pltpu.make_async_copy(source, heads.at[:, at], sems.at[4 + i]))
    early = len(copies)
    for i in range(4):
        ref = own_ref if i < 2 else other_ref
        part = ref.at[:, :, :, pl.ds((i % 2) * 256, 256)]
        copies.append(pltpu.make_async_copy(part, weights.at[i], sems.at[i]))
    for copy in copies:
        copy.start()
    for copy in copies[:early]:
        copy.wait()

    low = dot(down_ref[...], heads[...], ((1,), (1,)))
    low_bf = low.astype(bf16)
    low_ref[...] = low_bf
    stats[...] = jnp.zeros_like(stats)

    @pl.loop(0, 4)
    def _(step):
        pltpu.make_async_copy(weights.at[step], weights.at[step], sems.at[step]).wait()
        half = jnp.where(step < 2, core, 1 - core)
        at = pl.multiple_of(half * 512 + lax.rem(step, 2) * 256, 256)
        columns = pl.ds(at, 256)
        total = resid_ref[:, columns].astype(f32) + 2.0 * dot(
            low_bf, up_ref[:, columns], ((0,), (0,))
        )
        rows = jnp.concatenate(
            [
                weights[step, x * 4 + y, zl]
                for x in range(4)
                for zl in range(4)
                for y in range(4)
            ]
        )
        proj = dot(heads[...], rows, ((1,), (0,)))
        total += proj
        hidden_ref[:, columns] = total
        high, rest = split(total)
        row_high, row_rest = split(rows_ref[columns, :])
        inner = ((1,), (0,))
        products = dot(high, row_high, inner) + (
            dot(high, row_rest, inner) + dot(rest, row_high, inner)
        )
        square = total * total
        lane = lax.broadcasted_iota(jnp.int32, (tokens, 128), 1)
        sums = square[:, :128] + square[:, 128:]
        stats[...] += products + jnp.where(
            lane == 0, jnp.sum(sums, axis=1, keepdims=True), 0.0
        )

    stats_ref[...] = stats[...].T[:24]


def hidden_and_stats(place, heads, blocks, own, other, resid, down, up, rows):
    tokens, cols = heads.shape
    vmem = pl.BlockSpec(memory_space=pltpu.VMEM)
    hbm = pl.BlockSpec(memory_space=pl.ANY)
    smem = pl.BlockSpec(memory_space=pltpu.SMEM)
    return pl.pallas_call(
        hidden_kernel,
        out_shape=(
            jax.ShapeDtypeStruct((tokens, cols), f32),
            jax.ShapeDtypeStruct((16, tokens), bf16),
            jax.ShapeDtypeStruct((24, tokens), f32),
        ),
        in_specs=[smem] + [hbm] * 4 + [vmem] * 4,
        out_specs=(vmem, vmem, vmem),
        scratch_shapes=[
            pltpu.VMEM((tokens, 4 * cols), bf16),
            pltpu.VMEM((4, 16, 4, 64, 256), bf16),
            pltpu.VMEM((tokens, 128), f32),
            pltpu.SemaphoreType.DMA((8,)),
        ],
        compiler_params=pltpu.CompilerParams(vmem_limit_bytes=48 * 1024 * 1024),
        cost_estimate=pl.CostEstimate(
            flops=2 * tokens * 4096 * cols, bytes_accessed=16 * 2**20, transcendentals=0
        ),
    )(place, heads, blocks, own, other, resid, down, up, rows)


def shards(
    query_embedding_cache,
    passage_embedding_cache,
    positive,
    heads,
    residual,
    output_projection_weight,
    final_norm_gain,
    adapter_down_weight,
    adapter_up_weight,
    sequence_length,
):
    tokens, cols = heads.shape
    width = adapter_down_weight.shape[1]
    mp = lax.axis_index("mp")
    core = lax.axis_index("core")
    length = sequence_length[0]
    step = 32
    line, pairs = gather_line(
        output_projection_weight, query_embedding_cache, passage_embedding_cache, positive
    )
    rows, line = lax.optimization_barrier((heads, line))
    own = gather(line, ("x", "y")).reshape(16, 4, 64, 512)
    count = (length + step - 1) // step
    blocks = gather_valid(rows, count, step)
    own, blocks, pairs = lax.optimization_barrier((own, blocks, pairs))
    packed = spread(pairs, ("x", "y"), 16)
    other = lax.ppermute(own, "core", [(0, 1), (1, 0)])
    query_grad, passage_grad = pair_grads(
        query_embedding_cache, passage_embedding_cache, packed
    )
    upper = lax.dynamic_slice_in_dim(passage_grad, mp * cols, cols, 1)
    scaled = final_norm_gain[None, :] * upper

    up_wide = adapter_up_weight.astype(f32)
    scaled_up = jnp.sum(up_wide * scaled, axis=1)[None, :]
    hidden, low_bf, stats = hidden_and_stats(
        jnp.stack([mp, core]).astype(jnp.int32),
        heads,
        blocks,
        own,
        other,
        residual,
        adapter_down_weight,
        adapter_up_weight,
        jnp.pad(jnp.concatenate([scaled, up_wide]), ((1, 110), (0, 0))).T,
    )
    stats = jnp.concatenate(
        [
            stats[0:18],
            jnp.pad(scaled_up, ((0, 0), (0, tokens - 16))),
            jnp.zeros((5, tokens), f32),
        ]
    )
    stats = jnp.sum(spread(stats, "mp", 4).reshape(4, 24, tokens), axis=0)
    sumsq, dot_row, hidden_up = stats[0:1], stats[1:2], stats[2:18]
    scaled_up = stats[18, :16][:, None]
    inverse = lax.rsqrt(sumsq / width + norm_floor)
    factor = inverse**3 * dot_row / width
    positions = lax.broadcasted_iota(jnp.int32, (1, tokens), 1)
    mask = (positions < length).astype(f32) / length.astype(f32)
    low_grad = 2.0 * mask * (scaled_up * inverse - hidden_up * factor)
    down_term = dot(heads, low_grad.astype(bf16), ((0,), (1,)))
    low_wide = low_bf.astype(f32)
    hidden_grad = mask.reshape(tokens, 1) * (
        scaled * inverse.reshape(tokens, 1) - hidden * factor.reshape(tokens, 1)
    )
    up_term = 2.0 * dot(hidden_grad, low_wide, ((0,), (1,)), lax.Precision.HIGHEST)
    terms = jnp.concatenate([down_term, up_term], axis=1).reshape(128, 8, 32)
    terms = lax.all_to_all(terms, ("x", "zl"), 0, 0, tiled=True)
    terms = jnp.sum(terms.reshape(16, 8, 8, 32), axis=0)
    terms = jnp.sum(lax.all_to_all(terms, ("y", "core"), 0, 0, tiled=True), axis=0)
    return query_grad, passage_grad, terms[:, :16].T, terms[:, 16:].T


def solution(mesh):
    fine = Mesh(mesh.devices.reshape(SIZES), AXES)
    both = P(DP, "mp")
    placed = (
        P(DP, None),
        P(DP, None),
        P(DP),
        both,
        both,
        both,
        P("mp"),
        P(),
        P(None, "mp"),
        P(DP),
    )
    last = P(None, ("mp",) + DP)
    return jax.shard_map(
        shards,
        mesh=fine,
        in_specs=placed,
        out_specs=(P(DP, None), P(DP, None), last, last),
        check_vma=False,
    )
```
